32 devices in a mesh: pole: 2 (over y), row: 16 (over z, x, core).
Axes of the slice: x: 2, y: 2, z: 4, core: 2. Of those that a mesh axis runs over, the one named last changes fastest.
Arguments:
- inverse_rows: bfloat16 [4096, 2048], P(('pole', 'row')), parts along dimension 0, may hold values from -6 to 6
- lower_panels: bfloat16 [2, 4096, 384], P(None, ('pole', 'row')), parts along dimension 1, may hold values from -0.1875 to 0.1875
- link_block: bfloat16 [768, 384], P('pole'), parts along dimension 0, may hold values from -0.3125 to 0.3125
- diag_inverse: float32 [2, 768, 384], P(None, 'pole'), parts along dimension 1, may hold values from -6 to 6
- pattern: int32 [2, 32], replicated, may hold values from 0 to 1, as said below
Outputs:
- panel_first: bfloat16 [4096, 384], P(('pole', 'row')), parts along dimension 0
- panel_second: bfloat16 [4096, 384], P(('pole', 'row')), parts along dimension 0
- diag_first: float32 [768, 384], P('pole'), parts along dimension 0
- cross: float32 [768, 384], P('pole'), parts along dimension 0
- diag_second: float32 [768, 384], P('pole'), parts along dimension 0
The draws below stay inside these ranges and needn't reach their ends.
There are 2 independent parts, one for each index of `pole`. The reference program is written for one: setup_inputs(seed, part) draws one part's arguments, and reference() takes and returns one part's arrays. A program takes and returns all parts, laid end to end along the dimension named above; an argument that names none is the same for every part. Nothing has to cross between parts.
Inputs may be any that keep to these rules, and one draw needn't show every extreme that they name: `pattern`: each entry is 0 or 1. Among the 2 blocks of each aligned group (the blocks of one device), exactly 2 are marked in row 0 and exactly 1 in row 1; a block marked in row 1 is marked in row 0 too.
All inputs are finite; a program needn't handle non-finite values.
Results may differ from the reference program's by a relative error of at most 0.0043.
Values may be sent and summed in bfloat16 or wider, within the bound.
A program may use at most 128 MiB of HBM per device.

```python
import jax
import jax.numpy as jnp
from jax import lax

AW = 64
WK = 384
BLK_DEV = 2
KEEP_UP = 2
KEEP_LOW = 1
NB = 32
ROWS_U = 2048


def draw_pattern(key, part):
    key = jax.random.fold_in(key, 11)
    groups = NB // BLK_DEV
    keys = jax.random.split(key, groups)

    def ranking(single):
        return jax.random.permutation(single, BLK_DEV)
    ranks = jax.vmap(ranking)(keys)
    upper = (ranks < KEEP_UP).astype(jnp.int32).reshape(-1)
    lower = (ranks < KEEP_LOW).astype(jnp.int32).reshape(-1)
    return jnp.stack([upper, lower])


def shard_levels(rng, extent, cuts, smallest, top_value):
    gain, own = 1.0, jax.random.fold_in(rng, 6)
    for dim, blocks in cuts:
        steps = jnp.exp(jax.random.uniform(jax.random.fold_in(own, dim), (blocks,), jnp.float32, smallest / len(cuts), top_value / len(cuts)))
        gain = gain * jnp.repeat(steps, extent[dim] // blocks).reshape([-1 if axis == dim else 1 for axis in range(len(extent))])
    return gain


def centred(key, shape, scale, reach, cuts=(), kind=jnp.bfloat16):
    drawn = scale * jax.random.normal(key, shape, jnp.float32)
    if cuts:
        drawn = drawn * shard_levels(key, shape, cuts, -0.22, 0.18)
    return jnp.clip(drawn, -reach, reach).astype(kind)


def setup_inputs(seed: int = 0, part: int = 0) -> dict:
    splits = jax.random.split(jax.random.key(seed), 6)
    part_splits = jax.random.split(jax.random.fold_in(splits[5], part), 6)
    return {
        "inverse_rows": centred(part_splits[0], (ROWS_U, ROWS_U), 1.0, 6.0, ((0, 16),)),
        "lower_panels": centred(part_splits[1], (2, ROWS_U, WK), (ROWS_U // 2) ** -0.5, 0.1875, ((1, 16),)),
        "link_block": centred(part_splits[2], (WK, WK), WK ** -0.5, 0.3125),
        "diag_inverse": centred(part_splits[3], (2, WK, WK), 1.0, 6.0, (), jnp.float32),
        "pattern": draw_pattern(jax.random.fold_in(splits[5], 71), part),
    }


def reference(inverse_rows, lower_panels, link_block, diag_inverse, pattern):
    keep = jnp.repeat(pattern, AW, axis=1)
    keep_low = keep.astype(jnp.bfloat16)
    keep_wide = keep.astype(jnp.float32)
    first_masked = lower_panels[0] * keep_low[0][:, None]
    second_masked = lower_panels[1] * keep_low[1][:, None]
    far_first = jnp.dot(inverse_rows, first_masked, preferred_element_type=jnp.float32)
    panel_first = (-far_first * keep_wide[0][:, None]).astype(jnp.bfloat16)
    diag_first = diag_inverse[0] - jnp.dot(first_masked.T, panel_first, preferred_element_type=jnp.float32)
    far_second = jnp.dot(inverse_rows, second_masked, preferred_element_type=jnp.float32)
    near = jnp.dot(panel_first, link_block, preferred_element_type=jnp.float32)
    panel_second = (-(far_second + near) * keep_wide[1][:, None]).astype(jnp.bfloat16)
    link_wide = link_block.astype(jnp.float32)
    cross = -(jnp.dot(panel_first.T, second_masked, preferred_element_type=jnp.float32)
              + jnp.dot(diag_first, link_wide, precision=lax.Precision.HIGHEST))
    diag_second = (diag_inverse[1]
                   - jnp.dot(second_masked.T, panel_second, preferred_element_type=jnp.float32)
                   - jnp.dot(link_wide.T, cross, precision=lax.Precision.HIGHEST))
    return panel_first, panel_second, diag_first, cross, diag_second
```

```python
import functools

import jax
import jax.numpy as jnp
from jax import lax
from jax.experimental import pallas as pl
from jax.experimental.pallas import tpu as pltpu
from jax.sharding import PartitionSpec as P

AW = 64
MESH = pl.DeviceIdType.MESH
F32 = jnp.float32
BF16 = jnp.bfloat16


def dot(a, b):
    return jnp.dot(a, b, preferred_element_type=F32)


def dot_t(a, b):
    return lax.dot_general(a, b, (((0,), (0,)), ((), ())), preferred_element_type=F32)


def split2(x):
    hi = x.astype(BF16)
    lo = (x - hi.astype(F32)).astype(BF16)
    return hi, lo


def kernel(nz, pat, a_hbm, lp_hbm, l_hbm, d_hbm,
           p1_out, p2_out, d1_out, c_out, d2_out,
           a_v, g_v, h_v, su_v, sloc, l_v, d_v, p2_v,
           acc1, acc2, accd, accc, accs,
           in_sem, out_sem, z_send, x_send, c_send, recv):
    me = lax.axis_index("row")
    z = lax.div(me, 4)
    x = lax.rem(lax.div(me, 2), 2)
    c = lax.rem(me, 2)
    ox, oc = 1 - x, 1 - c

    def idx(zz, xx, cc):
        return (zz * 2 + xx) * 2 + cc

    cp_f = pltpu.make_async_copy(lp_hbm.at[0], g_v.at[me, pl.ds(0, 2 * AW)], in_sem.at[0])
    cp_s = pltpu.make_async_copy(lp_hbm.at[1], sloc, in_sem.at[1])
    cp_a = pltpu.make_async_copy(a_hbm, a_v, in_sem.at[2])
    cp_l = pltpu.make_async_copy(l_hbm, l_v, in_sem.at[3])
    cp_d = pltpu.make_async_copy(d_hbm, d_v, in_sem.at[4])
    for cp in (cp_f, cp_s, cp_a, cp_l, cp_d):
        cp.start()

    barrier = pltpu.get_barrier_semaphore()
    for target in (idx(z, ox, c), idx(z, x, oc)):
        pl.semaphore_signal(barrier, inc=1, device_id={"row": target}, device_id_type=MESH)

    @pl.when(z > 0)
    def _():
        pl.semaphore_signal(barrier, inc=1, device_id={"row": idx(z - 1, x, c)}, device_id_type=MESH)

    @pl.when(z < nz - 1)
    def _():
        pl.semaphore_signal(barrier, inc=1, device_id={"row": idx(z + 1, x, c)}, device_id_type=MESH)

    acc1[...] = jnp.zeros_like(acc1)
    acc2[...] = jnp.zeros_like(acc2)
    accd[...] = jnp.zeros_like(accd)
    accc[...] = jnp.zeros_like(accc)
    accs[...] = jnp.zeros_like(accs)

    low0 = pat[1, 2 * me]
    low1 = pat[1, 2 * me + 1]
    up0 = pat[0, 2 * me]
    up1 = pat[0, 2 * me + 1]

    def keep(mark, value):
        return jnp.where(mark != 0, value, jnp.zeros_like(value))

    cp_f.wait()
    for i, mark in enumerate((up0, up1)):
        rows = pl.ds(i * AW, AW)
        g_v[me, rows, :] = keep(mark, g_v[me, rows, :])
    cp_s.wait()
    g_v[me, pl.ds(2 * AW, AW), :] = jnp.where(low0 != 0, sloc[pl.ds(0, AW), :], sloc[pl.ds(AW, AW), :])

    pl.semaphore_wait(barrier, 2 + (z > 0).astype(jnp.int32) + (z < nz - 1).astype(jnp.int32))

    def remote(ph, buf, slot, send_sem, target):
        return pltpu.make_async_remote_copy(
            src_ref=buf.at[slot], dst_ref=buf.at[slot],
            send_sem=send_sem, recv_sem=recv.at[ph, slot],
            device_id={"row": target}, device_id_type=MESH)

    def zcopy(ph, buf, zz, way):
        return remote(ph, buf, idx(zz, x, c), z_send.at[ph, (way + 1) // 2, zz], idx(z + way, x, c))

    def xcopy(ph, buf, zz):
        return remote(ph, buf, idx(zz, x, c), x_send.at[ph, zz], idx(z, ox, c))

    def ccopy(ph, buf, zz, xx):
        return remote(ph, buf, idx(zz, xx, c), c_send.at[ph, zz * 2 + xx], idx(z, x, oc))

    def arrived(ph, buf, slot):
        remote(ph, buf, slot, c_send.at[ph, 0], idx(z, x, oc)).wait_recv()

    def inside(v):
        return jnp.logical_and(v >= 0, v < nz)

    def gather(ph, buf, pair):
        for way in (-1, 1):
            @pl.when(inside(z + way))
            def _():
                zcopy(ph, buf, z, way).start()
        xcopy(ph, buf, z).start()
        ccopy(ph, buf, z, x).start()

        def zstage(d, way):
            zz = z + way * d

            @pl.when(inside(zz))
            def _():
                arrived(ph, buf, idx(zz, x, c))

                @pl.when(inside(z - way))
                def _():
                    zcopy(ph, buf, zz, -way).start()
                xcopy(ph, buf, zz).start()
                ccopy(ph, buf, zz, x).start()

        def xstage(zz):
            arrived(ph, buf, idx(zz, ox, c))
            ccopy(ph, buf, zz, ox).start()

        def cstage(zz):
            arrived(ph, buf, idx(zz, x, oc))
            pair(zz * 2 + x)
            arrived(ph, buf, idx(zz, ox, oc))
            pair(zz * 2 + ox)

        zstage(1, -1)
        zstage(1, 1)
        xstage(z)
        cstage(z)

        def step(d, carry):
            zstage(d, -1)
            zstage(d, 1)
            for way in (-1, 1):
                zz = z + way * (d - 1)

                @pl.when(inside(zz))
                def _():
                    xstage(zz)
            for way in (-1, 1):
                zz = z + way * (d - 1)

                @pl.when(inside(zz))
                def _():
                    cstage(zz)
            return carry

        lax.fori_loop(2, nz + 1, step, 0)

    def drain(ph, buf):
        def step(zz, carry):
            for way in (-1, 1):
                sends = zz <= z if way == 1 else zz >= z

                @pl.when(jnp.logical_and(sends, inside(z + way)))
                def _():
                    zcopy(ph, buf, zz, way).wait_send()
            xcopy(ph, buf, zz).wait_send()
            ccopy(ph, buf, zz, 0).wait_send()
            ccopy(ph, buf, zz, 1).wait_send()
            return carry

        lax.fori_loop(0, nz, step, 0)

    cp_a.wait()
    cp_l.wait()
    cp_d.wait()

    width = l_v.shape[1]

    def f_pair(buf, p):
        return buf[pl.ds(2 * p, 2), pl.ds(0, 2 * AW), :].reshape(4 * AW, width)

    def s_pair(buf, p):
        return buf[pl.ds(2 * p, 2), pl.ds(2 * AW, AW), :].reshape(2 * AW, width)

    def pair_a(p):
        start = pl.multiple_of(p * 4 * AW, 4 * AW)
        a = a_v[:, pl.ds(start, 4 * AW)]
        acc1[...] += dot(a, f_pair(g_v, p))
        for i in range(4):
            su_v[pl.ds(pl.multiple_of(start + i * AW, AW), AW), :] = keep(
                pat[1, 4 * p + i], g_v[2 * p + i // 2, pl.ds(2 * AW, AW), :])
        acc2[...] += dot(a, su_v[pl.ds(start, 4 * AW), :])

    gather(0, g_v, pair_a)

    for i, mark in enumerate((up0, up1)):
        rows = pl.ds(i * AW, AW)
        h_v[me, rows, :] = keep(mark, (-acc1[rows, :])).astype(BF16)
    p1 = h_v[me, pl.ds(0, 2 * AW), :]
    far = -(acc2[...] + dot(p1, l_v[...]))
    far = far.astype(BF16)
    p2_v[pl.ds(0, AW), :] = keep(low0, far[:AW])
    p2_v[pl.ds(AW, AW), :] = keep(low1, far[AW:])
    h_v[me, pl.ds(2 * AW, AW), :] = jnp.where(low0 != 0, far[:AW], far[AW:])

    out1 = pltpu.make_async_copy(h_v.at[me, pl.ds(0, 2 * AW)], p1_out, out_sem.at[0])
    out2 = pltpu.make_async_copy(p2_v, p2_out, out_sem.at[1])
    out1.start()
    out2.start()

    def pair_b(p):
        start = pl.multiple_of(p * 4 * AW, 4 * AW)
        p1 = f_pair(h_v, p)
        accd[...] += dot_t(f_pair(g_v, p), p1)
        accc[...] += dot_t(p1, su_v[pl.ds(start, 4 * AW), :])
        accs[...] += dot_t(s_pair(g_v, p), s_pair(h_v, p))

    gather(1, h_v, pair_b)

    link = l_v[...]
    accd[...] = d_v[0] - accd[...]
    out3 = pltpu.make_async_copy(accd, d1_out, out_sem.at[2])
    out3.start()
    hi, lo = split2(accd[...])
    accc[...] = -(accc[...] + (dot(hi, link) + dot(lo, link)))
    out4 = pltpu.make_async_copy(accc, c_out, out_sem.at[3])
    out4.start()
    hi, lo = split2(accc[...])
    accs[...] = d_v[1] - accs[...] - (dot_t(link, hi) + dot_t(link, lo))
    out5 = pltpu.make_async_copy(accs, d2_out, out_sem.at[4])
    out5.start()
    drain(0, g_v)
    drain(1, h_v)
    for cp in (out1, out2, out3, out4, out5):
        cp.wait()


def shards(n, inverse_rows, lower_panels, link_block, diag_inverse, pattern):
    rows, total = inverse_rows.shape
    width = lower_panels.shape[2]
    nz = n // 4
    any_spec = pl.BlockSpec(memory_space=pl.ANY)
    out = jax.ShapeDtypeStruct
    return pl.pallas_call(
        functools.partial(kernel, nz),
        out_shape=(
            out((rows, width), BF16), out((rows, width), BF16),
            out((width, width), F32), out((width, width), F32), out((width, width), F32)),
        in_specs=[pl.BlockSpec(memory_space=pltpu.SMEM)] + [any_spec] * 4,
        out_specs=(any_spec,) * 5,
        scratch_shapes=[
            pltpu.VMEM((rows, total), BF16),
            pltpu.VMEM((n, 3 * AW, width), BF16),
            pltpu.VMEM((n, 3 * AW, width), BF16),
            pltpu.VMEM((total, width), BF16),
            pltpu.VMEM((rows, width), BF16),
            pltpu.VMEM((width, width), BF16),
            pltpu.VMEM((2, width, width), F32),
            pltpu.VMEM((rows, width), BF16),
            pltpu.VMEM((rows, width), F32),
            pltpu.VMEM((rows, width), F32),
            pltpu.VMEM((width, width), F32),
            pltpu.VMEM((width, width), F32),
            pltpu.VMEM((width, width), F32),
            pltpu.SemaphoreType.DMA((5,)),
            pltpu.SemaphoreType.DMA((5,)),
            pltpu.SemaphoreType.DMA((2, 2, nz)),
            pltpu.SemaphoreType.DMA((2, nz)),
            pltpu.SemaphoreType.DMA((2, 2 * nz)),
            pltpu.SemaphoreType.DMA((2, n)),
        ],
        compiler_params=pltpu.CompilerParams(
            collective_id=0, has_side_effects=True,
            vmem_limit_bytes=(62 if n > 32 else 32) * 2 ** 20),
    )(pattern, inverse_rows, lower_panels, link_block, diag_inverse)


def solution(mesh):
    in_specs = (
        P(("pole", "row"), None),
        P(None, ("pole", "row"), None),
        P("pole", None),
        P(None, "pole", None),
        P(),
    )
    out_specs = (
        P(("pole", "row"), None),
        P(("pole", "row"), None),
        P("pole", None),
        P("pole", None),
        P("pole", None),
    )
    return jax.shard_map(
        functools.partial(shards, mesh.shape["row"]), mesh=mesh,
        in_specs=in_specs, out_specs=out_specs, check_vma=False)
```

```python
import functools

import jax
import jax.numpy as jnp
from jax import lax
from jax.experimental import pallas as pl
from jax.experimental.pallas import tpu as pltpu
from jax.sharding import PartitionSpec as P

AW = 64
MESH = pl.DeviceIdType.MESH
F32 = jnp.float32
BF16 = jnp.bfloat16


def dot(a, b):
    return jnp.dot(a, b, preferred_element_type=F32)


def dot_t(a, b):
    return lax.dot_general(a, b, (((0,), (0,)), ((), ())), preferred_element_type=F32)


def split2(x):
    hi = x.astype(BF16)
    lo = (x - hi.astype(F32)).astype(BF16)
    return hi, lo


def kernel(nz, pat, a_hbm, lp_hbm, l_hbm, d_hbm,
           p1_out, p2_out, d1_out, c_out, d2_out,
           a_v, f_v, s_v, p_v, q_v, su_v, sloc, l_v, d_v,
           acc1, acc2, accd, accc, accs,
           in_sem, z_send, x_send, c_send, recv):
    me = lax.axis_index("row")
    z = lax.div(me, 4)
    x = lax.rem(lax.div(me, 2), 2)
    c = lax.rem(me, 2)
    ox, oc = 1 - x, 1 - c
    width = l_v.shape[1]
    bufs = (f_v, s_v, p_v, q_v)
    upper, lower, first, second = range(4)

    def idx(zz, xx, cc):
        return (zz * 2 + xx) * 2 + cc

    cp_f = pltpu.make_async_copy(lp_hbm.at[0], f_v.at[me], in_sem.at[0])
    cp_s = pltpu.make_async_copy(lp_hbm.at[1], sloc, in_sem.at[1])
    cp_a = pltpu.make_async_copy(a_hbm, a_v, in_sem.at[2])
    cp_l = pltpu.make_async_copy(l_hbm, l_v, in_sem.at[3])
    cp_d = pltpu.make_async_copy(d_hbm, d_v, in_sem.at[4])
    for cp in (cp_f, cp_s, cp_a, cp_l, cp_d):
        cp.start()

    def inside(v):
        return jnp.logical_and(v >= 0, v < nz)

    barrier = pltpu.get_barrier_semaphore()
    for target in (idx(z, ox, c), idx(z, x, oc)):
        pl.semaphore_signal(barrier, inc=1, device_id={"row": target}, device_id_type=MESH)
    for way in (-1, 1):
        @pl.when(inside(z + way))
        def _():
            pl.semaphore_signal(barrier, inc=1, device_id={"row": idx(z + way, x, c)}, device_id_type=MESH)

    low0, low1 = pat[1, 2 * me], pat[1, 2 * me + 1]
    up0, up1 = pat[0, 2 * me], pat[0, 2 * me + 1]

    def keep(mark, value):
        return jnp.where(mark != 0, value, jnp.zeros_like(value))

    cp_f.wait()
    for i, mark in enumerate((up0, up1)):
        rows = pl.ds(i * AW, AW)
        f_v[me, rows, :] = keep(mark, f_v[me, rows, :])
    cp_s.wait()
    s_v[me] = jnp.where(low0 != 0, sloc[pl.ds(0, AW), :], sloc[pl.ds(AW, AW), :])

    pl.semaphore_wait(barrier, 2 + (z > 0).astype(jnp.int32) + (z < nz - 1).astype(jnp.int32))

    def remote(st, slot, send_sem, target):
        return pltpu.make_async_remote_copy(
            src_ref=bufs[st].at[slot], dst_ref=bufs[st].at[slot],
            send_sem=send_sem, recv_sem=recv.at[st, slot],
            device_id={"row": target}, device_id_type=MESH)

    def zcopy(st, zz, way):
        return remote(st, idx(zz, x, c), z_send.at[st, (way + 1) // 2, zz], idx(z + way, x, c))

    def xcopy(st, zz):
        return remote(st, idx(zz, x, c), x_send.at[st, zz], idx(z, ox, c))

    def ccopy(st, zz, xx):
        return remote(st, idx(zz, xx, c), c_send.at[st, zz * 2 + xx], idx(z, x, oc))

    def arrived(st, slot):
        remote(st, slot, c_send.at[st, 0], idx(z, x, oc)).wait_recv()

    def send_own(st):
        for way in (-1, 1):
            @pl.when(inside(z + way))
            def _():
                zcopy(st, z, way).start()
        xcopy(st, z).start()
        ccopy(st, z, x).start()

    def at_distance(d, do):
        for way in (-1, 1):
            @pl.when(inside(z + way * d))
            def _():
                do(z + way * d, way)

    def relay(st, zz, way):
        arrived(st, idx(zz, x, c))

        @pl.when(inside(z - way))
        def _():
            zcopy(st, zz, -way).start()

    def across(st, zz):
        xcopy(st, zz).start()
        ccopy(st, zz, x).start()

    def from_x(st, zz):
        arrived(st, idx(zz, ox, c))
        ccopy(st, zz, ox).start()

    def from_core(st, zz, pair):
        arrived(st, idx(zz, x, oc))
        pair(zz * 2 + x)
        arrived(st, idx(zz, ox, oc))
        pair(zz * 2 + ox)

    def gather(one, two, pair_one):
        def z_one(zz, way):
            relay(one, zz, way)
            across(one, zz)

        def z_two(zz, way):
            relay(two, zz, way)

        at_distance(1, z_one)
        at_distance(1, z_two)
        from_x(one, z)
        from_core(one, z, pair_one)

        def step(d, carry):
            at_distance(d, z_one)
            at_distance(d - 1, lambda zz, way: across(two, zz))
            at_distance(d, z_two)
            at_distance(d - 1, lambda zz, way: from_x(one, zz))
            at_distance(d - 1, lambda zz, way: from_core(one, zz, pair_one))
            return carry

        lax.fori_loop(2, nz + 1, step, 0)

    def finish(two, pair_two):
        from_x(two, z)

        def turn(d, carry):
            at_distance(d, lambda zz, way: from_x(two, zz))
            return carry

        lax.fori_loop(1, nz, turn, 0)
        from_core(two, z, pair_two)

        def turn_core(d, carry):
            at_distance(d, lambda zz, way: from_core(two, zz, pair_two))
            return carry

        lax.fori_loop(1, nz, turn_core, 0)

    def columns(p):
        return pl.multiple_of(p * 4 * AW, 4 * AW)

    def pair_of(buf, p):
        return buf[pl.ds(2 * p, 2)].reshape(2 * buf.shape[1], width)

    def pair_upper(p):
        acc1[...] += dot(a_v[:, pl.ds(columns(p), 4 * AW)], pair_of(f_v, p))

    def pair_lower(p):
        start = columns(p)
        for i in range(4):
            su_v[pl.ds(pl.multiple_of(start + i * AW, AW), AW), :] = keep(
                pat[1, 4 * p + i], s_v[2 * p + i // 2])
        acc2[...] += dot(a_v[:, pl.ds(start, 4 * AW)], su_v[pl.ds(start, 4 * AW), :])

    def pair_first(p):
        p1 = pair_of(p_v, p)
        accd[...] += dot_t(pair_of(f_v, p), p1)
        accc[...] += dot_t(p1, su_v[pl.ds(columns(p), 4 * AW), :])

    def pair_second(p):
        accs[...] += dot_t(pair_of(s_v, p), pair_of(q_v, p))

    send_own(upper)
    send_own(lower)
    for acc in (acc1, acc2, accd, accc, accs):
        acc[...] = jnp.zeros_like(acc)
    cp_a.wait()
    cp_l.wait()
    cp_d.wait()

    gather(upper, lower, pair_upper)
    for i, mark in enumerate((up0, up1)):
        rows = pl.ds(i * AW, AW)
        p_v[me, rows, :] = keep(mark, -acc1[rows, :]).astype(BF16)
    send_own(first)

    p1 = p_v[me]
    p1_out[...] = p1
    acc2[...] += dot(p1, l_v[...])
    finish(lower, pair_lower)
    far = (-acc2[...]).astype(BF16)
    q_v[me] = jnp.where(low0 != 0, far[:AW], far[AW:])
    send_own(second)
    p2_out[pl.ds(0, AW), :] = keep(low0, far[:AW])
    p2_out[pl.ds(AW, AW), :] = keep(low1, far[AW:])

    gather(first, second, pair_first)
    link = l_v[...]
    diag = d_v[0] - accd[...]
    d1_out[...] = diag
    hi, lo = split2(diag)
    cross = -(accc[...] + (dot(hi, link) + dot(lo, link)))
    c_out[...] = cross
    hi, lo = split2(cross)
    accs[...] = (dot_t(link, hi) + dot_t(link, lo)) - d_v[1]
    finish(second, pair_second)
    d2_out[...] = -accs[...]

    def drain(zz, carry):
        for st in range(4):
            for way in (-1, 1):
                sends = zz <= z if way == 1 else zz >= z

                @pl.when(jnp.logical_and(sends, inside(z + way)))
                def _():
                    zcopy(st, zz, way).wait_send()
            xcopy(st, zz).wait_send()
            ccopy(st, zz, 0).wait_send()
            ccopy(st, zz, 1).wait_send()
        return carry

    lax.fori_loop(0, nz, drain, 0)


def write_out(*refs):
    for source, target in zip(refs[:5], refs[5:]):
        target[...] = source[...]


def shards(n, inverse_rows, lower_panels, link_block, diag_inverse, pattern):
    rows, total = inverse_rows.shape
    width = lower_panels.shape[2]
    nz = n // 4
    any_spec = pl.BlockSpec(memory_space=pl.ANY)
    out = jax.ShapeDtypeStruct
    shapes = (
            out((rows, width), BF16), out((rows, width), BF16),
            out((width, width), F32), out((width, width), F32), out((width, width), F32))
    made = pl.pallas_call(
        functools.partial(kernel, nz),
        out_shape=shapes,
        in_specs=[pl.BlockSpec(memory_space=pltpu.SMEM)] + [pl.BlockSpec(memory_space=pltpu.HBM)] * 4,
        out_specs=(pl.BlockSpec(memory_space=pltpu.VMEM),) * 5,
        scratch_shapes=[
            pltpu.VMEM((rows, total), BF16),
            pltpu.VMEM((n, rows, width), BF16),
            pltpu.VMEM((n, AW, width), BF16),
            pltpu.VMEM((n, rows, width), BF16),
            pltpu.VMEM((n, AW, width), BF16),
            pltpu.VMEM((total, width), BF16),
            pltpu.VMEM((rows, width), BF16),
            pltpu.VMEM((width, width), BF16),
            pltpu.VMEM((2, width, width), F32),
            pltpu.VMEM((rows, width), F32),
            pltpu.VMEM((rows, width), F32),
            pltpu.VMEM((width, width), F32),
            pltpu.VMEM((width, width), F32),
            pltpu.VMEM((width, width), F32),
            pltpu.SemaphoreType.DMA((5,)),
            pltpu.SemaphoreType.DMA((4, 2, nz)),
            pltpu.SemaphoreType.DMA((4, nz)),
            pltpu.SemaphoreType.DMA((4, 2 * nz)),
            pltpu.SemaphoreType.DMA((4, n)),
        ],
        compiler_params=pltpu.CompilerParams(
            collective_id=0, has_side_effects=True,
            vmem_limit_bytes=60 * 2 ** 20),
    )(pattern, inverse_rows, lower_panels, link_block, diag_inverse)
    return pl.pallas_call(
        write_out,
        out_shape=shapes,
        in_specs=[pl.BlockSpec(memory_space=pltpu.VMEM)] * 5,
        out_specs=(pl.BlockSpec(memory_space=pltpu.VMEM),) * 5,
    )(*made)


def solution(mesh):
    in_specs = (
        P(("pole", "row"), None),
        P(None, ("pole", "row"), None),
        P("pole", None),
        P(None, "pole", None),
        P(),
    )
    out_specs = (
        P(("pole", "row"), None),
        P(("pole", "row"), None),
        P("pole", None),
        P("pole", None),
        P("pole", None),
    )
    return jax.shard_map(
        functools.partial(shards, mesh.shape["row"]), mesh=mesh,
        in_specs=in_specs, out_specs=out_specs, check_vma=False)
```

```python
import functools

import jax
import jax.numpy as jnp
from jax import lax
from jax.experimental import pallas as pl
from jax.experimental.pallas import tpu as pltpu
from jax.sharding import PartitionSpec as P

AW = 64
MESH = pl.DeviceIdType.MESH
F32 = jnp.float32
BF16 = jnp.bfloat16


def dot(a, b):
    return jnp.dot(a, b, preferred_element_type=F32)


def dot_t(a, b):
    return lax.dot_general(a, b, (((0,), (0,)), ((), ())), preferred_element_type=F32)


def split2(x):
    hi = x.astype(BF16)
    lo = (x - hi.astype(F32)).astype(BF16)
    return hi, lo


def kernel(nz, pat, a_hbm, lp_hbm, l_hbm, d_hbm,
           p1_out, p2_out, d1_out, c_out, d2_out,
           a_v, f_v, s_v, p_v, q_v, su_v, sloc, l_v, d_v,
           acc1, acc2, accd, accc, accs,
           in_sem, z_send, x_send, c_send, recv):
    me = lax.axis_index("row")
    z = lax.div(me, 4)
    x = lax.rem(lax.div(me, 2), 2)
    c = lax.rem(me, 2)
    ox, oc = 1 - x, 1 - c
    width = l_v.shape[1]
    pieces = ((f_v, 0), (f_v, AW), (s_v, 0), (p_v, 0), (p_v, AW), (q_v, 0))
    upper, lower, first, second = (0, 1), (2,), (3, 4), (5,)

    def idx(zz, xx, cc):
        return (zz * 2 + xx) * 2 + cc

    cp_f = pltpu.make_async_copy(lp_hbm.at[0], f_v.at[me], in_sem.at[0])
    cp_s = pltpu.make_async_copy(lp_hbm.at[1], sloc, in_sem.at[1])
    cp_a = pltpu.make_async_copy(a_hbm, a_v, in_sem.at[2])
    cp_l = pltpu.make_async_copy(l_hbm, l_v, in_sem.at[3])
    cp_d = pltpu.make_async_copy(d_hbm, d_v, in_sem.at[4])
    for cp in (cp_f, cp_s, cp_a, cp_l, cp_d):
        cp.start()

    def inside(v):
        return jnp.logical_and(v >= 0, v < nz)

    barrier = pltpu.get_barrier_semaphore()
    for target in (idx(z, ox, c), idx(z, x, oc)):
        pl.semaphore_signal(barrier, inc=1, device_id={"row": target}, device_id_type=MESH)
    for way in (-1, 1):
        @pl.when(inside(z + way))
        def _():
            pl.semaphore_signal(barrier, inc=1, device_id={"row": idx(z + way, x, c)}, device_id_type=MESH)

    low0, low1 = pat[1, 2 * me], pat[1, 2 * me + 1]
    up0, up1 = pat[0, 2 * me], pat[0, 2 * me + 1]

    def keep(mark, value):
        return jnp.where(mark != 0, value, jnp.zeros_like(value))

    cp_f.wait()
    for i, mark in enumerate((up0, up1)):
        rows = pl.ds(i * AW, AW)
        f_v[me, rows, :] = keep(mark, f_v[me, rows, :])
    cp_s.wait()
    s_v[me] = jnp.where(low0 != 0, sloc[pl.ds(0, AW), :], sloc[pl.ds(AW, AW), :])

    pl.semaphore_wait(barrier, 2 + (z > 0).astype(jnp.int32) + (z < nz - 1).astype(jnp.int32))

    def remote(st, slot, send_sem, target):
        buf, start = pieces[st]
        rows = buf.at[slot, pl.ds(start, AW)]
        return pltpu.make_async_remote_copy(
            src_ref=rows, dst_ref=rows,
            send_sem=send_sem, recv_sem=recv.at[st, slot],
            device_id={"row": target}, device_id_type=MESH)

    def zcopy(st, zz, way):
        return remote(st, idx(zz, x, c), z_send.at[st, (way + 1) // 2, zz], idx(z + way, x, c))

    def xcopy(st, zz):
        return remote(st, idx(zz, x, c), x_send.at[st, zz], idx(z, ox, c))

    def ccopy(st, zz, xx):
        return remote(st, idx(zz, xx, c), c_send.at[st, zz * 2 + xx], idx(z, x, oc))

    def arrived(st, slot):
        remote(st, slot, c_send.at[st, 0], idx(z, x, oc)).wait_recv()

    def send_own(st):
        for way in (-1, 1):
            @pl.when(inside(z + way))
            def _():
                for piece in st:
                    zcopy(piece, z, way).start()
        across(st, z)

    def at_distance(d, do):
        for way in (-1, 1):
            @pl.when(inside(z + way * d))
            def _():
                do(z + way * d, way)

    def across(st, zz):
        for piece in st:
            xcopy(piece, zz).start()
            ccopy(piece, zz, x).start()

    def relay(st, zz, way, on):
        for piece in st:
            arrived(piece, idx(zz, x, c))

            @pl.when(inside(z - way))
            def _():
                zcopy(piece, zz, -way).start()
            if on:
                across((piece,), zz)

    def from_x(st, zz):
        for piece in st:
            arrived(piece, idx(zz, ox, c))
            ccopy(piece, zz, ox).start()

    def from_core(st, zz, pair):
        for xx in (x, ox):
            for piece in st:
                arrived(piece, idx(zz, xx, oc))
            pair(zz * 2 + xx)

    def gather(one, two, pair_one):
        def z_one(zz, way):
            relay(one, zz, way, True)

        def z_two(zz, way):
            relay(two, zz, way, False)

        at_distance(1, z_one)
        at_distance(1, z_two)
        from_x(one, z)
        from_core(one, z, pair_one)

        def step(d, carry):
            at_distance(d, z_one)
            at_distance(d - 1, lambda zz, way: across(two, zz))
            at_distance(d, z_two)
            at_distance(d - 1, lambda zz, way: from_x(one, zz))
            at_distance(d - 1, lambda zz, way: from_core(one, zz, pair_one))
            return carry

        lax.fori_loop(2, nz + 1, step, 0)

    def finish(two, pair_two):
        from_x(two, z)

        def turn(d, carry):
            at_distance(d, lambda zz, way: from_x(two, zz))
            return carry

        lax.fori_loop(1, nz, turn, 0)
        from_core(two, z, pair_two)

        def turn_core(d, carry):
            at_distance(d, lambda zz, way: from_core(two, zz, pair_two))
            return carry

        lax.fori_loop(1, nz, turn_core, 0)

    def columns(p):
        return pl.multiple_of(p * 4 * AW, 4 * AW)

    def pair_of(buf, p):
        return buf[pl.ds(2 * p, 2)].reshape(2 * buf.shape[1], width)

    def pair_upper(p):
        acc1[...] += dot(a_v[:, pl.ds(columns(p), 4 * AW)], pair_of(f_v, p))

    def pair_lower(p):
        start = columns(p)
        for i in range(4):
            su_v[pl.ds(pl.multiple_of(start + i * AW, AW), AW), :] = keep(
                pat[1, 4 * p + i], s_v[2 * p + i // 2])
        acc2[...] += dot(a_v[:, pl.ds(start, 4 * AW)], su_v[pl.ds(start, 4 * AW), :])

    def pair_first(p):
        p1 = pair_of(p_v, p)
        accd[...] += dot_t(pair_of(f_v, p), p1)
        accc[...] += dot_t(p1, su_v[pl.ds(columns(p), 4 * AW), :])

    def pair_second(p):
        accs[...] += dot_t(pair_of(s_v, p), pair_of(q_v, p))

    send_own(upper)
    send_own(lower)
    for acc in (acc1, acc2, accd, accc, accs):
        acc[...] = jnp.zeros_like(acc)
    cp_a.wait()
    cp_l.wait()
    cp_d.wait()

    gather(upper, lower, pair_upper)
    for i, mark in enumerate((up0, up1)):
        rows = pl.ds(i * AW, AW)
        p_v[me, rows, :] = keep(mark, -acc1[rows, :]).astype(BF16)
    send_own(first)

    p1 = p_v[me]
    p1_out[...] = p1
    acc2[...] += dot(p1, l_v[...])
    finish(lower, pair_lower)
    far = (-acc2[...]).astype(BF16)
    q_v[me] = jnp.where(low0 != 0, far[:AW], far[AW:])
    send_own(second)
    p2_out[pl.ds(0, AW), :] = keep(low0, far[:AW])
    p2_out[pl.ds(AW, AW), :] = keep(low1, far[AW:])

    gather(first, second, pair_first)
    link = l_v[...]
    diag = d_v[0] - accd[...]
    d1_out[...] = diag
    hi, lo = split2(diag)
    cross = -(accc[...] + (dot(hi, link) + dot(lo, link)))
    c_out[...] = cross
    hi, lo = split2(cross)
    accs[...] = (dot_t(link, hi) + dot_t(link, lo)) - d_v[1]
    finish(second, pair_second)
    d2_out[...] = -accs[...]

    def drain(zz, carry):
        for st in range(6):
            for way in (-1, 1):
                sends = zz <= z if way == 1 else zz >= z

                @pl.when(jnp.logical_and(sends, inside(z + way)))
                def _():
                    zcopy(st, zz, way).wait_send()
            xcopy(st, zz).wait_send()
            ccopy(st, zz, 0).wait_send()
            ccopy(st, zz, 1).wait_send()
        return carry

    lax.fori_loop(0, nz, drain, 0)


def write_out(*refs):
    for source, target in zip(refs[:5], refs[5:]):
        target[...] = source[...]


def shards(n, inverse_rows, lower_panels, link_block, diag_inverse, pattern):
    rows, total = inverse_rows.shape
    width = lower_panels.shape[2]
    nz = n // 4
    any_spec = pl.BlockSpec(memory_space=pl.ANY)
    out = jax.ShapeDtypeStruct
    shapes = (
            out((rows, width), BF16), out((rows, width), BF16),
            out((width, width), F32), out((width, width), F32), out((width, width), F32))
    made = pl.pallas_call(
        functools.partial(kernel, nz),
        out_shape=shapes,
        in_specs=[pl.BlockSpec(memory_space=pltpu.SMEM)] + [pl.BlockSpec(memory_space=pltpu.HBM)] * 4,
        out_specs=(pl.BlockSpec(memory_space=pltpu.VMEM),) * 5,
        scratch_shapes=[
            pltpu.VMEM((rows, total), BF16),
            pltpu.VMEM((n, rows, width), BF16),
            pltpu.VMEM((n, AW, width), BF16),
            pltpu.VMEM((n, rows, width), BF16),
            pltpu.VMEM((n, AW, width), BF16),
            pltpu.VMEM((total, width), BF16),
            pltpu.VMEM((rows, width), BF16),
            pltpu.VMEM((width, width), BF16),
            pltpu.VMEM((2, width, width), F32),
            pltpu.VMEM((rows, width), F32),
            pltpu.VMEM((rows, width), F32),
            pltpu.VMEM((width, width), F32),
            pltpu.VMEM((width, width), F32),
            pltpu.VMEM((width, width), F32),
            pltpu.SemaphoreType.DMA((5,)),
            pltpu.SemaphoreType.DMA((6, 2, nz)),
            pltpu.SemaphoreType.DMA((6, nz)),
            pltpu.SemaphoreType.DMA((6, 2 * nz)),
            pltpu.SemaphoreType.DMA((6, n)),
        ],
        compiler_params=pltpu.CompilerParams(
            collective_id=0, has_side_effects=True,
            vmem_limit_bytes=60 * 2 ** 20),
    )(pattern, inverse_rows, lower_panels, link_block, diag_inverse)
    return pl.pallas_call(
        write_out,
        out_shape=shapes,
        in_specs=[pl.BlockSpec(memory_space=pltpu.VMEM)] * 5,
        out_specs=(pl.BlockSpec(memory_space=pltpu.VMEM),) * 5,
    )(*made)


def solution(mesh):
    in_specs = (
        P(("pole", "row"), None),
        P(None, ("pole", "row"), None),
        P("pole", None),
        P(None, "pole", None),
        P(),
    )
    out_specs = (
        P(("pole", "row"), None),
        P(("pole", "row"), None),
        P("pole", None),
        P("pole", None),
        P("pole", None),
    )
    return jax.shard_map(
        functools.partial(shards, mesh.shape["row"]), mesh=mesh,
        in_specs=in_specs, out_specs=out_specs, check_vma=False)
```

```python
import functools

import jax
import jax.numpy as jnp
from jax import lax
from jax.experimental import pallas as pl
from jax.experimental.pallas import tpu as pltpu
from jax.sharding import PartitionSpec as P

AW = 64
MESH = pl.DeviceIdType.MESH
F32 = jnp.float32
BF16 = jnp.bfloat16


def dot(a, b):
    return jnp.dot(a, b, preferred_element_type=F32)


def dot_t(a, b):
    return lax.dot_general(a, b, (((0,), (0,)), ((), ())), preferred_element_type=F32)


def split2(x):
    hi = x.astype(BF16)
    lo = (x - hi.astype(F32)).astype(BF16)
    return hi, lo


def kernel(nz, pat, a_hbm, lp_hbm, l_hbm, d_hbm,
           p1_out, p2_out, d1_out, c_out, d2_out,
           a_v, f_v, s_v, p_v, q_v, su_v, sloc, l_v, d_v,
           acc1, acc2, accd, accc, accs,
           in_sem, z_send, x_send, c_send, recv):
    me = lax.axis_index("row")
    z = lax.div(me, 4)
    x = lax.rem(lax.div(me, 2), 2)
    c = lax.rem(me, 2)
    ox, oc = 1 - x, 1 - c
    width = l_v.shape[1]
    pieces = ((f_v, 0), (f_v, AW), (s_v, 0), (p_v, 0), (p_v, AW), (q_v, 0))
    upper, lower, first, second = (0, 1), (2,), (3, 4), (5,)

    def idx(zz, xx, cc):
        return (zz * 2 + xx) * 2 + cc

    cp_f = pltpu.make_async_copy(lp_hbm.at[0], f_v.at[me], in_sem.at[0])
    cp_s = pltpu.make_async_copy(lp_hbm.at[1], sloc, in_sem.at[1])
    cp_a = pltpu.make_async_copy(a_hbm, a_v, in_sem.at[2])
    cp_l = pltpu.make_async_copy(l_hbm, l_v, in_sem.at[3])
    cp_d = pltpu.make_async_copy(d_hbm, d_v, in_sem.at[4])
    for cp in (cp_f, cp_s, cp_a, cp_l, cp_d):
        cp.start()

    def inside(v):
        return jnp.logical_and(v >= 0, v < nz)

    barrier = pltpu.get_barrier_semaphore()
    for target in (idx(z, ox, c), idx(z, x, oc)):
        pl.semaphore_signal(barrier, inc=1, device_id={"row": target}, device_id_type=MESH)
    for way in (-1, 1):
        @pl.when(inside(z + way))
        def _():
            pl.semaphore_signal(barrier, inc=1, device_id={"row": idx(z + way, x, c)}, device_id_type=MESH)

    low0, low1 = pat[1, 2 * me], pat[1, 2 * me + 1]
    up0, up1 = pat[0, 2 * me], pat[0, 2 * me + 1]

    def keep(mark, value):
        return jnp.where(mark != 0, value, jnp.zeros_like(value))

    cp_f.wait()
    for i, mark in enumerate((up0, up1)):
        rows = pl.ds(i * AW, AW)
        f_v[me, rows, :] = keep(mark, f_v[me, rows, :])
    cp_s.wait()
    s_v[me] = jnp.where(low0 != 0, sloc[pl.ds(0, AW), :], sloc[pl.ds(AW, AW), :])

    pl.semaphore_wait(barrier, 2 + (z > 0).astype(jnp.int32) + (z < nz - 1).astype(jnp.int32))

    def remote(st, slot, send_sem, target):
        buf, start = pieces[st]
        rows = buf.at[slot, pl.ds(start, AW)]
        return pltpu.make_async_remote_copy(
            src_ref=rows, dst_ref=rows,
            send_sem=send_sem, recv_sem=recv.at[st, slot],
            device_id={"row": target}, device_id_type=MESH)

    def zcopy(st, zz, way):
        return remote(st, idx(zz, x, c), z_send.at[st, (way + 1) // 2, zz], idx(z + way, x, c))

    def xcopy(st, zz):
        return remote(st, idx(zz, x, c), x_send.at[st, zz], idx(z, ox, c))

    def ccopy(st, zz, xx):
        return remote(st, idx(zz, xx, c), c_send.at[st, zz * 2 + xx], idx(z, x, oc))

    def arrived(st, slot):
        remote(st, slot, c_send.at[st, 0], idx(z, x, oc)).wait_recv()

    def send_own(st):
        for way in (-1, 1):
            @pl.when(inside(z + way))
            def _():
                for piece in st:
                    zcopy(piece, z, way).start()
        across(st, z)

    def at_distance(d, do):
        for way in (-1, 1):
            @pl.when(inside(z + way * d))
            def _():
                do(z + way * d, way)

    def across(st, zz):
        for piece in st:
            xcopy(piece, zz).start()
            ccopy(piece, zz, x).start()

    def relay(st, zz, way, on):
        for piece in st:
            arrived(piece, idx(zz, x, c))

            @pl.when(inside(z - way))
            def _():
                zcopy(piece, zz, -way).start()
            if on:
                across((piece,), zz)

    def from_x(st, zz):
        for piece in st:
            arrived(piece, idx(zz, ox, c))
            ccopy(piece, zz, ox).start()

    def from_core(st, zz, pair):
        for xx in (x, ox):
            for piece in st:
                arrived(piece, idx(zz, xx, oc))
            pair(zz * 2 + xx)

    def gather(one, two, pair_one, begun):
        def z_one(zz, way):
            relay(one, zz, way, True)

        def z_two(zz, way):
            relay(two, zz, way, False)

        if not begun:
            at_distance(1, z_one)
        at_distance(1, z_two)
        from_x(one, z)
        from_core(one, z, pair_one)

        def step(d, carry):
            at_distance(d, z_one)
            at_distance(d - 1, lambda zz, way: across(two, zz))
            at_distance(d, z_two)
            at_distance(d - 1, lambda zz, way: from_x(one, zz))
            at_distance(d - 1, lambda zz, way: from_core(one, zz, pair_one))
            return carry

        lax.fori_loop(2, nz + 1, step, 0)

    def finish(two, pair_two, following):
        from_x(two, z)

        def turn(d, carry):
            at_distance(d, lambda zz, way: from_x(two, zz))
            return carry

        lax.fori_loop(1, nz, turn, 0)
        if following:
            at_distance(1, lambda zz, way: relay(following, zz, way, True))
        from_core(two, z, pair_two)

        def turn_core(d, carry):
            at_distance(d, lambda zz, way: from_core(two, zz, pair_two))
            return carry

        lax.fori_loop(1, nz, turn_core, 0)

    def columns(p):
        return pl.multiple_of(p * 4 * AW, 4 * AW)

    def pair_of(buf, p):
        return buf[pl.ds(2 * p, 2)].reshape(2 * buf.shape[1], width)

    def pair_upper(p):
        acc1[...] += dot(a_v[:, pl.ds(columns(p), 4 * AW)], pair_of(f_v, p))

    def pair_lower(p):
        start = columns(p)
        for i in range(4):
            su_v[pl.ds(pl.multiple_of(start + i * AW, AW), AW), :] = keep(
                pat[1, 4 * p + i], s_v[2 * p + i // 2])
        acc2[...] += dot(a_v[:, pl.ds(start, 4 * AW)], su_v[pl.ds(start, 4 * AW), :])

    def pair_first(p):
        p1 = pair_of(p_v, p)
        accd[...] += dot_t(pair_of(f_v, p), p1)
        accc[...] += dot_t(p1, su_v[pl.ds(columns(p), 4 * AW), :])

    def pair_second(p):
        accs[...] += dot_t(pair_of(s_v, p), pair_of(q_v, p))

    send_own(upper)
    send_own(lower)
    for acc in (acc1, acc2, accd, accc, accs):
        acc[...] = jnp.zeros_like(acc)
    cp_a.wait()
    cp_l.wait()
    cp_d.wait()

    gather(upper, lower, pair_upper, False)
    for i, mark in enumerate((up0, up1)):
        rows = pl.ds(i * AW, AW)
        p_v[me, rows, :] = keep(mark, -acc1[rows, :]).astype(BF16)
    send_own(first)

    p1 = p_v[me]
    p1_out[...] = p1
    acc2[...] += dot(p1, l_v[...])
    finish(lower, pair_lower, first)
    far = (-acc2[...]).astype(BF16)
    q_v[me] = jnp.where(low0 != 0, far[:AW], far[AW:])
    send_own(second)
    p2_out[pl.ds(0, AW), :] = keep(low0, far[:AW])
    p2_out[pl.ds(AW, AW), :] = keep(low1, far[AW:])

    gather(first, second, pair_first, True)
    link = l_v[...]
    diag = d_v[0] - accd[...]
    d1_out[...] = diag
    hi, lo = split2(diag)
    cross = -(accc[...] + (dot(hi, link) + dot(lo, link)))
    c_out[...] = cross
    hi, lo = split2(cross)
    accs[...] = (dot_t(link, hi) + dot_t(link, lo)) - d_v[1]
    finish(second, pair_second, ())
    d2_out[...] = -accs[...]

    def drain(zz, carry):
        for st in range(6):
            for way in (-1, 1):
                sends = zz <= z if way == 1 else zz >= z

                @pl.when(jnp.logical_and(sends, inside(z + way)))
                def _():
                    zcopy(st, zz, way).wait_send()
            xcopy(st, zz).wait_send()
            ccopy(st, zz, 0).wait_send()
            ccopy(st, zz, 1).wait_send()
        return carry

    lax.fori_loop(0, nz, drain, 0)


def write_out(*refs):
    for source, target in zip(refs[:5], refs[5:]):
        target[...] = source[...]


def shards(n, inverse_rows, lower_panels, link_block, diag_inverse, pattern):
    rows, total = inverse_rows.shape
    width = lower_panels.shape[2]
    nz = n // 4
    any_spec = pl.BlockSpec(memory_space=pl.ANY)
    out = jax.ShapeDtypeStruct
    shapes = (
            out((rows, width), BF16), out((rows, width), BF16),
            out((width, width), F32), out((width, width), F32), out((width, width), F32))
    made = pl.pallas_call(
        functools.partial(kernel, nz),
        out_shape=shapes,
        in_specs=[pl.BlockSpec(memory_space=pltpu.SMEM)] + [pl.BlockSpec(memory_space=pltpu.HBM)] * 4,
        out_specs=(pl.BlockSpec(memory_space=pltpu.VMEM),) * 5,
        scratch_shapes=[
            pltpu.VMEM((rows, total), BF16),
            pltpu.VMEM((n, rows, width), BF16),
            pltpu.VMEM((n, AW, width), BF16),
            pltpu.VMEM((n, rows, width), BF16),
            pltpu.VMEM((n, AW, width), BF16),
            pltpu.VMEM((total, width), BF16),
            pltpu.VMEM((rows, width), BF16),
            pltpu.VMEM((width, width), BF16),
            pltpu.VMEM((2, width, width), F32),
            pltpu.VMEM((rows, width), F32),
            pltpu.VMEM((rows, width), F32),
            pltpu.VMEM((width, width), F32),
            pltpu.VMEM((width, width), F32),
            pltpu.VMEM((width, width), F32),
            pltpu.SemaphoreType.DMA((5,)),
            pltpu.SemaphoreType.DMA((6, 2, nz)),
            pltpu.SemaphoreType.DMA((6, nz)),
            pltpu.SemaphoreType.DMA((6, 2 * nz)),
            pltpu.SemaphoreType.DMA((6, n)),
        ],
        compiler_params=pltpu.CompilerParams(
            collective_id=0, has_side_effects=True,
            vmem_limit_bytes=60 * 2 ** 20),
    )(pattern, inverse_rows, lower_panels, link_block, diag_inverse)
    return pl.pallas_call(
        write_out,
        out_shape=shapes,
        in_specs=[pl.BlockSpec(memory_space=pltpu.VMEM)] * 5,
        out_specs=(pl.BlockSpec(memory_space=pltpu.VMEM),) * 5,
    )(*made)


def solution(mesh):
    in_specs = (
        P(("pole", "row"), None),
        P(None, ("pole", "row"), None),
        P("pole", None),
        P(None, "pole", None),
        P(),
    )
    out_specs = (
        P(("pole", "row"), None),
        P(("pole", "row"), None),
        P("pole", None),
        P("pole", None),
        P("pole", None),
    )
    return jax.shard_map(
        functools.partial(shards, mesh.shape["row"]), mesh=mesh,
        in_specs=in_specs, out_specs=out_specs, check_vma=False)
```
